768 devices in a mesh: dp: 96 (over y_hi, z, core), outer: 8 (over x, y_lo).
Axes of the slice: x: 4, y: 8 (y_hi: 4, y_lo: 2; y = y_hi * 2 + y_lo), z: 12, core: 2. Of those that a mesh axis runs over, the one named last changes fastest.
Arguments:
- grads: bfloat16 [8, 96, 192, 4096], P('outer', 'dp'), may hold values from -20 to 20
- momentum: float32 [8, 192, 4096], P('outer', 'dp'), may hold values from -6 to 6
- corner: int32 [192, 2], P('dp'), may hold values from 0 to 8
Outputs:
- new_momentum: float32 [8, 192, 4096], P('outer', 'dp')
- update: float32 [192, 4096], P('dp')
The draws below stay inside these ranges and needn't reach their ends.
All inputs are finite; a program needn't handle non-finite values.
Results may differ from the reference program's by a relative error of at most 0.0003.
Values sent between devices are 32-bit elements; how exact they have to be, the bound alone decides.
No kernel may reach another device: no remote copies, remote signals or barrier semaphores. Data moves between devices by JAX's collectives and lax.ppermute only.
A program may use at most 32 MiB of HBM per device.

```python
import math
import jax
import jax.numpy as jnp
from jax import lax

SPAN = 64
CORNER = 8
SPANS = 192
N_DP = 96
N_OUTER = 8


def plant(result, rng, least, largest):
    longest = result.shape.index(max(result.shape))
    spots = []
    for shift in (0, 1):
        where = [jax.random.randint(jax.random.fold_in(rng, axis), (), 0, length) for axis, length in enumerate(result.shape)]
        where[longest] = (where[longest] + shift) % result.shape[longest]
        spots.append(tuple(where))
    return result.at[spots[0]].set(least).at[spots[1]].set(largest)


def strengthened(result, rng, source, target, parts, factor):
    owner, partner = [(jnp.arange(result.shape[position]) // (result.shape[position] // parts)).reshape([-1 if axis == position else 1 for axis in range(result.ndim)]) for position in (source, target)]
    chosen = jax.random.permutation(rng, parts)[partner]
    strong = (owner == chosen) | (owner == (partner + parts // 2) % parts)
    return jnp.where(strong, factor * result, result)


def steps_of(stream_key, extent, cuts, low, top_value):
    def one(dim, parts):
        heights = jax.random.uniform(jax.random.fold_in(jax.random.fold_in(stream_key, 6), dim), (parts,), jnp.float32, low / len(cuts), top_value / len(cuts))
        return jnp.repeat(jnp.exp(heights), extent[dim] // parts).reshape((-1,) + (1,) * (len(extent) - dim - 1))

    gain = one(*cuts[0])
    for cut in cuts[1:]:
        gain = gain * one(*cut)
    return gain


def normal_values(own_key, extent, spread, most, split=(), held_as=jnp.bfloat16):
    values = spread * jax.random.normal(own_key, extent, jnp.float32)
    if split:
        values = values * steps_of(own_key, extent, split, -0.22, 0.18)
    return jnp.clip(values, -most, most).astype(held_as)


def bell_draw_with(own_key, shape, spread, reach, shards, heavy, held_as=jnp.bfloat16):
    result = spread * jax.random.normal(own_key, shape, jnp.float32)
    if shards:
        result = result * steps_of(own_key, shape, shards, -0.22, 0.18)
    return jnp.clip(strengthened(result, jax.random.fold_in(own_key, 3), *heavy), -reach, reach).astype(held_as)


def setup_inputs(seed: int = 0) -> dict:
    arg_keys = jax.random.split(jax.random.key(seed), 4)
    return {
        "grads": bell_draw_with(arg_keys[0], (N_OUTER, N_DP, SPANS, SPAN * SPAN), 1.0, 20.0, ((0, 8), (1, 96)), (1, 2, 96, 4.75)),
        "momentum": normal_values(arg_keys[1], (N_OUTER, SPANS, SPAN * SPAN), 1.0, 6.0, ((0, 8), (1, 96)), jnp.float32),
        "corner": plant(jax.random.randint(arg_keys[2], (SPANS, 2), 0, SPAN // 8 + 1), jax.random.fold_in(arg_keys[2], 1), 0, (SPAN // 8 + 1) - 1).astype(jnp.int32),
    }


def cosine_table(length):
    freq = jnp.arange(length, dtype=jnp.float32)[:, None]
    place = jnp.arange(length, dtype=jnp.float32)[None, :]
    factor = jnp.where(freq == 0, math.sqrt(1.0 / length), math.sqrt(2.0 / length))
    return (factor * jnp.cos(math.pi * (2.0 * place + 1.0) * freq / (2.0 * length))).astype(jnp.float32)

def pickers(corner):
    across = jnp.arange(SPAN, dtype=jnp.int32)[None, None, :]
    inside = jnp.arange(CORNER, dtype=jnp.int32)[None, :, None]
    row_pick = (across == corner[:, 0][:, None, None] + inside).astype(jnp.float32)
    col_pick = (across == corner[:, 1][:, None, None] + inside).astype(jnp.float32)
    return (row_pick, col_pick)

def forward_corner(blocks, table, row_pick, col_pick):
    high = lax.Precision.HIGHEST
    square = blocks.reshape(blocks.shape[0], SPAN, SPAN)
    coeffs = jnp.einsum('ij,kjl,ml->kim', table, square, table, precision=high)
    left = jnp.einsum('kaj,kjl->kal', row_pick, coeffs, precision=high)
    return jnp.einsum('kal,kbl->kab', left, col_pick, precision=high)

def inverse_corner(kept, table, row_pick, col_pick):
    high = lax.Precision.HIGHEST
    placed = jnp.einsum('kaj,kab,kbl->kjl', row_pick, kept, col_pick, precision=high)
    square = jnp.einsum('ji,kjl,lm->kim', table, placed, table, precision=high)
    return square.reshape(kept.shape[0], SPAN * SPAN)

def reference(grads, momentum, corner):
    table = cosine_table(SPAN)
    row_pick, col_pick = pickers(corner)

    def add_one(index, total):
        piece = lax.dynamic_index_in_dim(grads, index, 1, keepdims=False)
        return total + piece.astype(jnp.float32)
    summed = lax.fori_loop(0, N_DP, add_one, jnp.zeros((N_OUTER, SPANS, SPAN * SPAN), jnp.float32))
    mean_grad = summed / N_DP
    moment = 0.9 * momentum + mean_grad
    kept = jax.vmap(lambda blocks: forward_corner(blocks, table, row_pick, col_pick))(moment)
    removed = jax.vmap(lambda part: inverse_corner(part, table, row_pick, col_pick))(kept)
    new_momentum = moment - removed
    average = lax.optimization_barrier(jnp.sum(kept, axis=0)) / N_OUTER
    update = inverse_corner(average, table, row_pick, col_pick)
    return (new_momentum, update)
```

```python
import math

import jax
import jax.numpy as jnp
import numpy as np
from jax import lax
from jax.experimental import pallas as pl
from jax.experimental.pallas import tpu as pltpu
from jax.sharding import PartitionSpec as P

SPAN = 64
CORNER = 8
LOW = 16
NY, NZ = 4, 12
N_DP = 96
N_OUTER = 8
HIGH = lax.Precision.HIGHEST


def device_of(y, z, core):
    return ((y % NY) * NZ + z % NZ) * 2 + core


def shift(dz=0, dcore=0):
    return [
        (device_of(y, z, c), device_of(y, z + dz, c ^ dcore))
        for y in range(NY)
        for z in range(NZ)
        for c in range(2)
    ]


def far_groups():
    return [
        [device_of(y, 3 * q + s, c) for q in range(4) for y in range(NY)]
        for s in range(3)
        for c in range(2)
    ]


def tables():
    k = np.arange(SPAN)[:, None]
    n = np.arange(SPAN)[None, :]
    scale = np.where(k == 0, math.sqrt(1.0 / SPAN), math.sqrt(2.0 / SPAN))
    full = scale * np.cos(np.pi * (2 * n + 1) * k / (2.0 * SPAN))
    low = full[:LOW]
    left = np.zeros((2, 2, LOW, 2, 32))
    for h in range(2):
        for b in range(2):
            left[h, b, :, b, :] = low[:, h::2]
    left = left.reshape(64, 64)
    right = np.zeros((128, 128))
    right[:, :LOW] = np.concatenate([low.T, low.T], axis=0)
    return tuple(np.asarray(v, np.float32) for v in (left, left.T, right, right.T))


def arrange_kernel(grads, send, own, square):
    place = lax.axis_index("dp")
    core = lax.rem(place, 2)
    z = lax.rem(place // 2, NZ)

    def spread(i, carry):
        rows = pl.multiple_of(i * 16, 16)
        for t in range(32):
            tile = grads[0, 0, pl.ds(rows, 16), t * 128 : (t + 1) * 128].astype(jnp.float32)
            square[pl.ds(rows * 32 + t, 16, stride=32), :] = tile
        return carry

    lax.fori_loop(0, 12, spread, 0)
    kinds = [lax.rem(z + d, 3) for d in (1, 2, 0)]

    def deal(i, carry):
        q, y = i // NY, lax.rem(i, NY)
        for slot, kind in enumerate(kinds):
            chip = y * NZ + 3 * q + kind
            for ref, c in ((send, 1 - core), (own, core)):
                first = pl.multiple_of((chip * 2 + c) * 64, 64)
                ref[slot, i] = square[pl.ds(first, 64), :]
        return carry

    lax.fori_loop(0, 16, deal, 0)


def arrange(grads):
    shape = jax.ShapeDtypeStruct((3, 16, 64, 128), jnp.float32)
    vmem = pl.BlockSpec(memory_space=pltpu.VMEM)
    return pl.pallas_call(
        arrange_kernel,
        out_shape=(shape, shape),
        in_specs=[vmem],
        out_specs=(vmem, vmem),
        scratch_shapes=[pltpu.VMEM((6144, 128), jnp.float32)],
        compiler_params=pltpu.CompilerParams(vmem_limit_bytes=24 << 20),
    )(grads)


def dot(a, b):
    return jnp.dot(a, b, precision=HIGH, preferred_element_type=jnp.float32)


def same_half():
    row = lax.broadcasted_iota(jnp.int32, (64, 128), 0)
    lane = lax.broadcasted_iota(jnp.int32, (64, 128), 1)
    return (row < 32) == (lane < 64)


def rebuild(low, left_t, right_t):
    wide = dot(low, right_t)
    both = jnp.where(same_half(), jnp.concatenate([wide, wide], axis=0), 0.0)
    return dot(left_t, both)


def kept_kernel(parts, momentum, corner, left, right, moment, packed, square):
    for t in range(32):
        square[pl.ds(t, 2, stride=32), :] = momentum[0, :, t * 128 : (t + 1) * 128]
    total = parts[0]
    for k in range(1, 16):
        total = total + parts[k]
    value = 0.9 * square[...] + total / N_DP
    moment[...] = value
    half = jnp.where(same_half(), dot(left[...], value), 0.0)
    mixed = dot(half, right[...])
    low = mixed[:32] + mixed[32:]
    row = lax.broadcasted_iota(jnp.int32, (32, 128), 0)
    lane = lax.broadcasted_iota(jnp.int32, (32, 128), 1)
    first = row < LOW
    place = jnp.where(first, row, row - LOW)
    above = place - jnp.where(first, corner[0, 0], corner[1, 0])
    beside = lane - jnp.where(first, corner[0, 1], corner[1, 1])
    inside = (above >= 0) & (above < CORNER) & (beside >= 0) & (beside < CORNER)
    kept = jnp.where(inside, low, 0.0)
    pack = kept[0:8]
    for g in range(1, 4):
        pack = pack + pltpu.roll(kept[8 * g : 8 * g + 8], 16 * g, axis=1)
    for p in range(N_OUTER):
        packed[p] = pack


def unpack(pack):
    lane = lax.broadcasted_iota(jnp.int32, (8, 128), 1)
    parts = [pack] + [pltpu.roll(pack, 128 - 16 * g, axis=1) for g in range(1, 4)]
    return jnp.concatenate([jnp.where(lane < LOW, v, 0.0) for v in parts], axis=0)


def momentum_kernel(moment, packed, left_t, right_t, out, square):
    square[...] = moment[...] - rebuild(unpack(packed[0]), left_t[...], right_t[...])
    for t in range(32):
        out[0, :, t * 128 : (t + 1) * 128] = square[pl.ds(t, 2, stride=32), :]


def update_kernel(packed, left_t, right_t, out, square):
    total = packed[0]
    for p in range(1, N_OUTER):
        total = total + packed[p]
    square[...] = rebuild(unpack(total / N_OUTER), left_t[...], right_t[...])
    for t in range(32):
        out[:, t * 128 : (t + 1) * 128] = square[pl.ds(t, 2, stride=32), :]


def on_device(grads, momentum, corner):
    left, left_t, right, right_t = (jnp.asarray(v) for v in tables())
    vmem = pl.BlockSpec(memory_space=pltpu.VMEM)
    smem = pl.BlockSpec(memory_space=pltpu.SMEM)
    square = pltpu.VMEM((64, 128), jnp.float32)

    send, own = arrange(grads)
    chip = own + lax.ppermute(send, "dp", shift(dcore=1))
    from_below = lax.ppermute(chip[0], "dp", shift(dz=1))
    from_above = lax.ppermute(chip[1], "dp", shift(dz=-1))
    near = chip[2] + from_below + from_above
    parts = lax.all_to_all(near, "dp", 0, 0, axis_index_groups=far_groups(), tiled=True)

    moment, packed = pl.pallas_call(
        kept_kernel,
        out_shape=(
            jax.ShapeDtypeStruct((64, 128), jnp.float32),
            jax.ShapeDtypeStruct((N_OUTER, 8, 128), jnp.float32),
        ),
        in_specs=[vmem, vmem, smem, vmem, vmem],
        out_specs=(vmem, vmem),
        scratch_shapes=[square],
    )(parts, momentum, corner, left, right)
    shared = lax.all_to_all(packed, "outer", 0, 0, tiled=True)
    new_momentum = pl.pallas_call(
        momentum_kernel,
        out_shape=jax.ShapeDtypeStruct((1, 2, 4096), jnp.float32),
        in_specs=[vmem] * 4,
        out_specs=vmem,
        scratch_shapes=[square],
    )(moment, packed, left_t, right_t)
    update = pl.pallas_call(
        update_kernel,
        out_shape=jax.ShapeDtypeStruct((2, 4096), jnp.float32),
        in_specs=[vmem] * 3,
        out_specs=vmem,
        scratch_shapes=[square],
    )(shared, left_t, right_t)
    return (new_momentum, update)


def solution(mesh):
    in_specs = (P("outer", "dp", None, None), P("outer", "dp", None), P("dp", None))
    out_specs = (P("outer", "dp", None), P("dp", None))
    return jax.shard_map(
        on_device, mesh=mesh, in_specs=in_specs, out_specs=out_specs, check_vma=False
    )
```

```python
import math

import jax
import jax.numpy as jnp
import ml_dtypes
import numpy as np
from jax import lax
from jax.experimental import pallas as pl
from jax.experimental.pallas import tpu as pltpu
from jax.sharding import PartitionSpec as P

SPAN = 64
CORNER = 8
LOW = 16
NY, NZ = 4, 12
N_DP = 96
N_OUTER = 8
VMEM = pl.BlockSpec(memory_space=pltpu.VMEM)
SMEM = pl.BlockSpec(memory_space=pltpu.SMEM)


def device_of(y, z, core):
    return ((y % NY) * NZ + z % NZ) * 2 + core


def shift(dz=0, dcore=0):
    return [
        (device_of(y, z, c), device_of(y, z + dz, c ^ dcore))
        for y in range(NY)
        for z in range(NZ)
        for c in range(2)
    ]


def y_groups():
    return [[device_of(y, z, c) for y in range(NY)] for z in range(NZ) for c in range(2)]


def z_groups():
    return [
        [device_of(y, 3 * q + s, c) for q in range(4)]
        for s in range(3)
        for y in range(NY)
        for c in range(2)
    ]


def halves(table):
    high = table.astype(ml_dtypes.bfloat16)
    low = (table - high.astype(np.float64)).astype(ml_dtypes.bfloat16)
    return high, low


def left_three(table):
    high, low = halves(table)
    return np.concatenate([high, low, high], axis=1)


def right_three(table):
    high, low = halves(table)
    return np.concatenate([high, low, high], axis=0)


def tables():
    k = np.arange(SPAN)[:, None]
    n = np.arange(SPAN)[None, :]
    scale = np.where(k == 0, math.sqrt(1.0 / SPAN), math.sqrt(2.0 / SPAN))
    low = (scale * np.cos(np.pi * (2 * n + 1) * k / (2.0 * SPAN)))[:LOW]
    left = np.zeros((2, 2, LOW, 2, 32))
    for h in range(2):
        for b in range(2):
            left[h, b, :, b, :] = low[:, h::2]
    left = left.reshape(64, 64)
    right = np.zeros((4, 128, 128))
    for g in range(4):
        right[g, :, 16 * g : 16 * g + 16] = np.concatenate([low.T, low.T], axis=0)
    right = right.reshape(512, 128)
    return left_three(left), right_three(right), left_three(left.T), right_three(right.T)


def chunk(y, q, kind, core):
    return pl.multiple_of(((y * NZ + 3 * q + kind) * 2 + core) * 64, 64)


def place():
    me = lax.axis_index("dp")
    core = lax.rem(me, 2)
    z = lax.rem(me // 2, NZ)
    return core, [lax.rem(z + d, 3) for d in (1, 2, 0)]


def arrange_kernel(grads, send, square):
    core, kinds = place()

    def spread(i, carry):
        rows = pl.multiple_of(i * 16, 16)
        for t in range(32):
            tile = grads[0, 0, pl.ds(rows, 16), t * 128 : (t + 1) * 128].astype(jnp.float32)
            square[pl.ds(rows * 32 + t, 16, stride=32), :] = tile
        return carry

    lax.fori_loop(0, 12, spread, 0)

    def deal(i, carry):
        y, q = i // 4, lax.rem(i, 4)
        for slot, kind in enumerate(kinds):
            send[slot, i] = square[pl.ds(chunk(y, q, kind, 1 - core), 64), :]
        return carry

    lax.fori_loop(0, 16, deal, 0)


def arrange(grads):
    shapes = [(3, 16, 64, 128), (6144, 128)]
    return pl.pallas_call(
        arrange_kernel,
        out_shape=tuple(jax.ShapeDtypeStruct(s, jnp.float32) for s in shapes),
        in_specs=[VMEM],
        out_specs=(VMEM, VMEM),
        compiler_params=pltpu.CompilerParams(vmem_limit_bytes=24 << 20),
    )(grads)


def chip_kernel(square, other, up, down, here):
    core, kinds = place()

    def add(i, carry):
        y, q = i // 4, lax.rem(i, 4)
        for slot, ref in enumerate((up, down, here)):
            mine = square[pl.ds(chunk(y, q, kinds[slot], core), 64), :]
            ref[i] = mine + other[slot, i]
        return carry

    lax.fori_loop(0, 16, add, 0)


def dot(a, b):
    return jnp.dot(a, b, preferred_element_type=jnp.float32)


def split(value):
    high = value.astype(jnp.bfloat16)
    low = (value - high.astype(jnp.float32)).astype(jnp.bfloat16)
    return high, low


def dot_left(table, value):
    high, low = split(value)
    return dot(table, jnp.concatenate([high, high, low], axis=0))


def dot_right(value, table):
    high, low = split(value)
    return dot(jnp.concatenate([high, high, low], axis=1), table)


def kept_kernel(parts, momentum, corner, left, right, moment, kept, copies, square):
    for t in range(32):
        square[pl.ds(t, 2, stride=32), :] = momentum[0, :, t * 128 : (t + 1) * 128]
    total = (parts[0] + parts[1]) + (parts[2] + parts[3])
    value = 0.9 * square[...] + total / N_DP
    moment[...] = value
    mixed = dot_left(left[...], value)
    lane = lax.broadcasted_iota(jnp.int32, (32, 128), 1)
    half = jnp.where(lane < SPAN, mixed[:32], mixed[32:])
    wide = jnp.concatenate([half[8 * g : 8 * g + 8] for g in range(4)], axis=1)
    low = dot_right(wide, right[...])
    row = lax.broadcasted_iota(jnp.int32, (8, 128), 0)
    lane = lax.broadcasted_iota(jnp.int32, (8, 128), 1)
    first = lane < 2 * LOW
    above = row + 8 * ((lane // LOW) % 2) - jnp.where(first, corner[0, 0], corner[1, 0])
    beside = lane % LOW - jnp.where(first, corner[0, 1], corner[1, 1])
    inside = (above >= 0) & (above < CORNER) & (beside >= 0) & (beside < CORNER)
    pack = jnp.where(inside & (lane < 4 * LOW), low, 0.0)
    kept[...] = pack
    for p in range(N_OUTER):
        copies[p] = pack


def last_kernel(moment, kept, packed, left_t, right_t, out, update, square, other):
    shared = packed[0]
    for p in range(1, N_OUTER):
        shared = shared + packed[p]
    both = jnp.concatenate([kept[...], shared / N_OUTER], axis=0)
    wide = dot_right(both, right_t[...])
    row = lax.broadcasted_iota(jnp.int32, (64, 128), 0)
    lane = lax.broadcasted_iota(jnp.int32, (64, 128), 1)
    same = (row < 32) == (lane < SPAN)
    sides = []
    for first in (0, 8):
        tall = [wide[first : first + 8, 128 * g : 128 * g + 128] for g in range(4)]
        sides.append(jnp.where(same, jnp.concatenate(tall + tall, axis=0), 0.0))
    back = dot_left(left_t[...], jnp.concatenate(sides, axis=1))
    square[...] = moment[...] - back[:, :128]
    other[...] = back[:, 128:]
    for t in range(32):
        out[0, :, t * 128 : (t + 1) * 128] = square[pl.ds(t, 2, stride=32), :]
        update[:, t * 128 : (t + 1) * 128] = other[pl.ds(t, 2, stride=32), :]


def call(kernel, out_shapes, args, scratch=(), smem=()):
    return pl.pallas_call(
        kernel,
        out_shape=tuple(jax.ShapeDtypeStruct(s, jnp.float32) for s in out_shapes),
        in_specs=[SMEM if i in smem else VMEM for i in range(len(args))],
        out_specs=tuple(VMEM for _ in out_shapes),
        scratch_shapes=[pltpu.VMEM(s, jnp.float32) for s in scratch],
        compiler_params=pltpu.CompilerParams(vmem_limit_bytes=24 << 20),
    )(*args)


def exchange(value, axis, groups=None):
    return lax.all_to_all(value, axis, 0, 0, axis_index_groups=groups, tiled=True)


def on_device(grads, momentum, corner):
    left, right, left_t, right_t = (jnp.asarray(v) for v in tables())
    tile = (64, 128)
    send, square = arrange(grads)
    other = lax.ppermute(send, "dp", shift(dcore=1))
    up, down, here = call(chip_kernel, [(16, 64, 128)] * 3, (square, other))
    from_below = lax.ppermute(up, "dp", shift(dz=1))
    from_above = lax.ppermute(down, "dp", shift(dz=-1))
    near = exchange(here + from_below + from_above, "dp", y_groups())
    line = near.reshape(NY, 4, 64, 128).sum(axis=0)
    parts = exchange(line, "dp", z_groups())
    moment, kept, copies = call(
        kept_kernel,
        [tile, (8, 128), (N_OUTER, 8, 128)],
        (parts, momentum, corner, left, right),
        [tile],
        smem=(2,),
    )
    packed = exchange(copies, "outer")
    return call(
        last_kernel,
        [(1, 2, 4096), (2, 4096)],
        (moment, kept, packed, left_t, right_t),
        [tile, tile],
    )


def solution(mesh):
    in_specs = (P("outer", "dp", None, None), P("outer", "dp", None), P("dp", None))
    out_specs = (P("outer", "dp", None), P("dp", None))
    return jax.shard_map(
        on_device, mesh=mesh, in_specs=in_specs, out_specs=out_specs, check_vma=False
    )
```

```python
import math

import jax
import jax.numpy as jnp
import ml_dtypes
import numpy as np
from jax import lax
from jax.experimental import pallas as pl
from jax.experimental.pallas import tpu as pltpu
from jax.sharding import PartitionSpec as P

SPAN = 64
CORNER = 8
LOW = 16
NY, NZ = 4, 12
N_DP = 96
N_OUTER = 8
VMEM = pl.BlockSpec(memory_space=pltpu.VMEM)
SMEM = pl.BlockSpec(memory_space=pltpu.SMEM)


def device_of(y, z, core):
    return ((y % NY) * NZ + z % NZ) * 2 + core


def shift(dz=0, dcore=0):
    return [
        (device_of(y, z, c), device_of(y, z + dz * (1 - 2 * c), c ^ dcore))
        for y in range(NY)
        for z in range(NZ)
        for c in range(2)
    ]


def y_groups():
    return [[device_of(y, z, c) for y in range(NY)] for z in range(NZ) for c in range(2)]


def z_groups():
    return [
        [device_of(y, 3 * q + s, c) for q in range(4)]
        for s in range(3)
        for y in range(NY)
        for c in range(2)
    ]


def halves(table):
    high = table.astype(ml_dtypes.bfloat16)
    low = (table - high.astype(np.float64)).astype(ml_dtypes.bfloat16)
    return high, low


def left_three(table):
    high, low = halves(table)
    return np.concatenate([high, low, high], axis=1)


def right_three(table):
    high, low = halves(table)
    return np.concatenate([high, low, high], axis=0)


def tables():
    k = np.arange(SPAN)[:, None]
    n = np.arange(SPAN)[None, :]
    scale = np.where(k == 0, math.sqrt(1.0 / SPAN), math.sqrt(2.0 / SPAN))
    low = (scale * np.cos(np.pi * (2 * n + 1) * k / (2.0 * SPAN)))[:LOW]
    left = np.zeros((2, 2, LOW, 2, 32))
    for h in range(2):
        for b in range(2):
            left[h, b, :, b, :] = low[:, h::2]
    left = left.reshape(64, 64)
    right = np.zeros((4, 128, 128))
    for g in range(4):
        right[g, :, 16 * g : 16 * g + 16] = np.concatenate([low.T, low.T], axis=0)
    right = right.reshape(512, 128)
    return left_three(left), right_three(right), left_three(left.T), right_three(right.T)


def chunk(y, q, kind, core):
    return pl.multiple_of(((y * NZ + 3 * q + kind) * 2 + core) * 64, 64)


def place():
    me = lax.axis_index("dp")
    core = lax.rem(me, 2)
    z = lax.rem(me // 2, NZ)
    return core, [lax.rem(z + d, 3) for d in (1 + core, 2 - core, 0)]


def arrange_kernel(grads, send, square):
    core, kinds = place()

    def spread(i, carry):
        rows = pl.multiple_of(i * 16, 16)
        for t in range(32):
            tile = grads[0, 0, pl.ds(rows, 16), t * 128 : (t + 1) * 128].astype(jnp.float32)
            square[pl.ds(rows * 32 + t, 16, stride=32), :] = tile
        return carry

    lax.fori_loop(0, 12, spread, 0)

    def deal(i, carry):
        y, q = i // 4, lax.rem(i, 4)
        for slot, kind in enumerate((kinds[1], kinds[0], kinds[2])):
            send[slot, i] = square[pl.ds(chunk(y, q, kind, 1 - core), 64), :]
        return carry

    lax.fori_loop(0, 16, deal, 0)


def arrange(grads):
    shapes = [(3, 16, 64, 128), (6144, 128)]
    return pl.pallas_call(
        arrange_kernel,
        out_shape=tuple(jax.ShapeDtypeStruct(s, jnp.float32) for s in shapes),
        in_specs=[VMEM],
        out_specs=(VMEM, VMEM),
        compiler_params=pltpu.CompilerParams(vmem_limit_bytes=24 << 20),
    )(grads)


def chip_kernel(square, other, first, second, here):
    core, kinds = place()

    def add(i, carry):
        y, q = i // 4, lax.rem(i, 4)
        for slot, ref in enumerate((first, second, here)):
            mine = square[pl.ds(chunk(y, q, kinds[slot], core), 64), :]
            ref[i] = mine + other[slot, i]
        return carry

    lax.fori_loop(0, 16, add, 0)


def dot(a, b):
    return jnp.dot(a, b, preferred_element_type=jnp.float32)


def split(value):
    high = value.astype(jnp.bfloat16)
    low = (value - high.astype(jnp.float32)).astype(jnp.bfloat16)
    return high, low


def dot_left(table, value):
    high, low = split(value)
    return dot(table, jnp.concatenate([high, high, low], axis=0))


def dot_right(value, table):
    high, low = split(value)
    return dot(jnp.concatenate([high, high, low], axis=1), table)


def kept_kernel(parts, momentum, corner, left, right, moment, kept, copies, square):
    for t in range(32):
        square[pl.ds(t, 2, stride=32), :] = momentum[0, :, t * 128 : (t + 1) * 128]
    total = (parts[0] + parts[1]) + (parts[2] + parts[3])
    value = 0.9 * square[...] + total / N_DP
    moment[...] = value
    mixed = dot_left(left[...], value)
    lane = lax.broadcasted_iota(jnp.int32, (32, 128), 1)
    half = jnp.where(lane < SPAN, mixed[:32], mixed[32:])
    wide = jnp.concatenate([half[8 * g : 8 * g + 8] for g in range(4)], axis=1)
    low = dot_right(wide, right[...])
    row = lax.broadcasted_iota(jnp.int32, (8, 128), 0)
    lane = lax.broadcasted_iota(jnp.int32, (8, 128), 1)
    first = lane < 2 * LOW
    above = row + 8 * ((lane // LOW) % 2) - jnp.where(first, corner[0, 0], corner[1, 0])
    beside = lane % LOW - jnp.where(first, corner[0, 1], corner[1, 1])
    inside = (above >= 0) & (above < CORNER) & (beside >= 0) & (beside < CORNER)
    pack = jnp.where(inside & (lane < 4 * LOW), low, 0.0)
    kept[...] = pack
    for p in range(N_OUTER):
        copies[p] = pack


def last_kernel(moment, kept, packed, left_t, right_t, out, update, square, other):
    shared = packed[0]
    for p in range(1, N_OUTER):
        shared = shared + packed[p]
    both = jnp.concatenate([kept[...], shared / N_OUTER], axis=0)
    wide = dot_right(both, right_t[...])
    row = lax.broadcasted_iota(jnp.int32, (64, 128), 0)
    lane = lax.broadcasted_iota(jnp.int32, (64, 128), 1)
    same = (row < 32) == (lane < SPAN)
    sides = []
    for first in (0, 8):
        tall = [wide[first : first + 8, 128 * g : 128 * g + 128] for g in range(4)]
        sides.append(jnp.where(same, jnp.concatenate(tall + tall, axis=0), 0.0))
    back = dot_left(left_t[...], jnp.concatenate(sides, axis=1))
    square[...] = moment[...] - back[:, :128]
    other[...] = back[:, 128:]
    for t in range(32):
        out[0, :, t * 128 : (t + 1) * 128] = square[pl.ds(t, 2, stride=32), :]
        update[:, t * 128 : (t + 1) * 128] = other[pl.ds(t, 2, stride=32), :]


def call(kernel, out_shapes, args, scratch=(), smem=()):
    return pl.pallas_call(
        kernel,
        out_shape=tuple(jax.ShapeDtypeStruct(s, jnp.float32) for s in out_shapes),
        in_specs=[SMEM if i in smem else VMEM for i in range(len(args))],
        out_specs=tuple(VMEM for _ in out_shapes),
        scratch_shapes=[pltpu.VMEM(s, jnp.float32) for s in scratch],
        compiler_params=pltpu.CompilerParams(vmem_limit_bytes=24 << 20),
    )(*args)


def exchange(value, axis, groups=None):
    return lax.all_to_all(value, axis, 0, 0, axis_index_groups=groups, tiled=True)


def on_device(grads, momentum, corner):
    left, right, left_t, right_t = (jnp.asarray(v) for v in tables())
    tile = (64, 128)
    send, square = arrange(grads)
    other = lax.ppermute(send, "dp", shift(dcore=1))
    first, second, here = call(chip_kernel, [(16, 64, 128)] * 3, (square, other))
    one = lax.ppermute(first, "dp", shift(dz=1))
    two = lax.ppermute(second, "dp", shift(dz=-1))
    near = exchange(here + one + two, "dp", y_groups())
    line = near.reshape(NY, 4, 64, 128).sum(axis=0)
    parts = exchange(line, "dp", z_groups())
    moment, kept, copies = call(
        kept_kernel,
        [tile, (8, 128), (N_OUTER, 8, 128)],
        (parts, momentum, corner, left, right),
        [tile],
        smem=(2,),
    )
    packed = exchange(copies, "outer")
    return call(
        last_kernel,
        [(1, 2, 4096), (2, 4096)],
        (moment, kept, packed, left_t, right_t),
        [tile, tile],
    )


def solution(mesh):
    in_specs = (P("outer", "dp", None, None), P("outer", "dp", None), P("dp", None))
    out_specs = (P("outer", "dp", None), P("dp", None))
    return jax.shard_map(
        on_device, mesh=mesh, in_specs=in_specs, out_specs=out_specs, check_vma=False
    )
```

```python
import math

import jax
import jax.numpy as jnp
import ml_dtypes
import numpy as np
from jax import lax
from jax.experimental import pallas as pl
from jax.experimental.pallas import tpu as pltpu
from jax.sharding import PartitionSpec as P

SPAN = 64
CORNER = 8
LOW = 16
NY, NZ = 4, 12
N_DP = 96
N_OUTER = 8
VMEM = pl.BlockSpec(memory_space=pltpu.VMEM)
SMEM = pl.BlockSpec(memory_space=pltpu.SMEM)


def device_of(y, z, core):
    return ((y % NY) * NZ + z % NZ) * 2 + core


def shift(dz=0, dcore=0):
    return [
        (device_of(y, z, c), device_of(y, z + dz * (1 - 2 * c), c ^ dcore))
        for y in range(NY)
        for z in range(NZ)
        for c in range(2)
    ]


def y_groups():
    return [[device_of(y, z, c) for y in range(NY)] for z in range(NZ) for c in range(2)]


def z_groups():
    return [
        [device_of(y, 3 * q + s, c) for q in range(4)]
        for s in range(3)
        for y in range(NY)
        for c in range(2)
    ]


def halves(table):
    high = table.astype(ml_dtypes.bfloat16)
    low = (table - high.astype(np.float64)).astype(ml_dtypes.bfloat16)
    return high, low


def left_three(table):
    high, low = halves(table)
    return np.concatenate([high, low, high], axis=1)


def right_three(table):
    high, low = halves(table)
    return np.concatenate([high, low, high], axis=0)


def tables():
    k = np.arange(SPAN)[:, None]
    n = np.arange(SPAN)[None, :]
    scale = np.where(k == 0, math.sqrt(1.0 / SPAN), math.sqrt(2.0 / SPAN))
    low = (scale * np.cos(np.pi * (2 * n + 1) * k / (2.0 * SPAN)))[:LOW]
    left = np.zeros((2, 2, LOW, 2, 32))
    for h in range(2):
        for b in range(2):
            left[h, b, :, b, :] = low[:, h::2]
    left = left.reshape(64, 64)
    right = np.zeros((4, 128, 128))
    for g in range(4):
        right[g, :, 16 * g : 16 * g + 16] = np.concatenate([low.T, low.T], axis=0)
    right = right.reshape(512, 128)
    return left_three(left), right_three(right), left_three(left.T), right_three(right.T)


def chunk(y, q, kind, core):
    return pl.multiple_of(((y * NZ + 3 * q + kind) * 2 + core) * 64, 64)


def place():
    me = lax.axis_index("dp")
    core = lax.rem(me, 2)
    z = lax.rem(me // 2, NZ)
    return core, [lax.rem(z + d, 3) for d in (1 + core, 2 - core, 0)]


def arrange_kernel(grads, send, square):
    core, kinds = place()

    def spread(i, carry):
        rows = pl.multiple_of(i * 16, 16)
        for first in range(0, 32, 8):
            wide = grads[0, 0, pl.ds(rows, 16), first * 128 : (first + 8) * 128]
            wide = wide.astype(jnp.float32)
            for side in (0, 8):
                turned = wide[side : side + 8].reshape(8, 8, 128)
                for r in range(8):
                    start = pl.multiple_of((rows + side + r) * 32 + first, 8)
                    square[pl.ds(start, 8), :] = turned[r]
        return carry

    lax.fori_loop(0, 12, spread, 0)

    def deal(i, carry):
        y, q = i // 4, lax.rem(i, 4)
        for slot, kind in enumerate((kinds[1], kinds[0], kinds[2])):
            send[slot, i] = square[pl.ds(chunk(y, q, kind, 1 - core), 64), :]
        return carry

    lax.fori_loop(0, 16, deal, 0)


def arrange(grads):
    shapes = [(3, 16, 64, 128), (6144, 128)]
    return pl.pallas_call(
        arrange_kernel,
        out_shape=tuple(jax.ShapeDtypeStruct(s, jnp.float32) for s in shapes),
        in_specs=[VMEM],
        out_specs=(VMEM, VMEM),
        compiler_params=pltpu.CompilerParams(vmem_limit_bytes=24 << 20),
    )(grads)


def chip_kernel(square, other, first, second, here):
    core, kinds = place()

    def add(i, carry):
        y, q = i // 4, lax.rem(i, 4)
        for slot, ref in enumerate((first, second, here)):
            mine = square[pl.ds(chunk(y, q, kinds[slot], core), 64), :]
            ref[i] = mine + other[slot, i]
        return carry

    lax.fori_loop(0, 16, add, 0)


def dot(a, b):
    return jnp.dot(a, b, preferred_element_type=jnp.float32)


def split(value):
    high = value.astype(jnp.bfloat16)
    low = (value - high.astype(jnp.float32)).astype(jnp.bfloat16)
    return high, low


def dot_left(table, value):
    high, low = split(value)
    return dot(table, jnp.concatenate([high, high, low], axis=0))


def dot_right(value, table):
    high, low = split(value)
    return dot(jnp.concatenate([high, high, low], axis=1), table)


def kept_kernel(parts, momentum, corner, left, right, moment, kept, copies, square):
    for t in range(32):
        square[pl.ds(t, 2, stride=32), :] = momentum[0, :, t * 128 : (t + 1) * 128]
    total = (parts[0] + parts[1]) + (parts[2] + parts[3])
    value = 0.9 * square[...] + total / N_DP
    moment[...] = value
    mixed = dot_left(left[...], value)
    lane = lax.broadcasted_iota(jnp.int32, (32, 128), 1)
    half = jnp.where(lane < SPAN, mixed[:32], mixed[32:])
    wide = jnp.concatenate([half[8 * g : 8 * g + 8] for g in range(4)], axis=1)
    low = dot_right(wide, right[...])
    row = lax.broadcasted_iota(jnp.int32, (8, 128), 0)
    lane = lax.broadcasted_iota(jnp.int32, (8, 128), 1)
    first = lane < 2 * LOW
    above = row + 8 * ((lane // LOW) % 2) - jnp.where(first, corner[0, 0], corner[1, 0])
    beside = lane % LOW - jnp.where(first, corner[0, 1], corner[1, 1])
    inside = (above >= 0) & (above < CORNER) & (beside >= 0) & (beside < CORNER)
    pack = jnp.where(inside & (lane < 4 * LOW), low, 0.0)
    kept[...] = pack
    for p in range(N_OUTER):
        copies[p] = pack


def last_kernel(moment, kept, packed, left_t, right_t, out, update, square, other):
    shared = packed[0]
    for p in range(1, N_OUTER):
        shared = shared + packed[p]
    both = jnp.concatenate([kept[...], shared / N_OUTER], axis=0)
    wide = dot_right(both, right_t[...])
    row = lax.broadcasted_iota(jnp.int32, (64, 128), 0)
    lane = lax.broadcasted_iota(jnp.int32, (64, 128), 1)
    same = (row < 32) == (lane < SPAN)
    sides = []
    for first in (0, 8):
        tall = [wide[first : first + 8, 128 * g : 128 * g + 128] for g in range(4)]
        sides.append(jnp.where(same, jnp.concatenate(tall + tall, axis=0), 0.0))
    back = dot_left(left_t[...], jnp.concatenate(sides, axis=1))
    square[...] = moment[...] - back[:, :128]
    other[...] = back[:, 128:]
    for t in range(32):
        out[0, :, t * 128 : (t + 1) * 128] = square[pl.ds(t, 2, stride=32), :]
        update[:, t * 128 : (t + 1) * 128] = other[pl.ds(t, 2, stride=32), :]


def call(kernel, out_shapes, args, scratch=(), smem=()):
    return pl.pallas_call(
        kernel,
        out_shape=tuple(jax.ShapeDtypeStruct(s, jnp.float32) for s in out_shapes),
        in_specs=[SMEM if i in smem else VMEM for i in range(len(args))],
        out_specs=tuple(VMEM for _ in out_shapes),
        scratch_shapes=[pltpu.VMEM(s, jnp.float32) for s in scratch],
        compiler_params=pltpu.CompilerParams(vmem_limit_bytes=24 << 20),
    )(*args)


def exchange(value, axis, groups=None):
    return lax.all_to_all(value, axis, 0, 0, axis_index_groups=groups, tiled=True)


def on_device(grads, momentum, corner):
    left, right, left_t, right_t = (jnp.asarray(v) for v in tables())
    tile = (64, 128)
    send, square = arrange(grads)
    other = lax.ppermute(send, "dp", shift(dcore=1))
    first, second, here = call(chip_kernel, [(16, 64, 128)] * 3, (square, other))
    one = lax.ppermute(first, "dp", shift(dz=1))
    two = lax.ppermute(second, "dp", shift(dz=-1))
    near = exchange(here + one + two, "dp", y_groups())
    line = near.reshape(NY, 4, 64, 128).sum(axis=0)
    parts = exchange(line, "dp", z_groups())
    moment, kept, copies = call(
        kept_kernel,
        [tile, (8, 128), (N_OUTER, 8, 128)],
        (parts, momentum, corner, left, right),
        [tile],
        smem=(2,),
    )
    packed = exchange(copies, "outer")
    return call(
        last_kernel,
        [(1, 2, 4096), (2, 4096)],
        (moment, kept, packed, left_t, right_t),
        [tile, tile],
    )


def solution(mesh):
    in_specs = (P("outer", "dp", None, None), P("outer", "dp", None), P("dp", None))
    out_specs = (P("outer", "dp", None), P("dp", None))
    return jax.shard_map(
        on_device, mesh=mesh, in_specs=in_specs, out_specs=out_specs, check_vma=False
    )
```

```python
import math

import jax
import jax.numpy as jnp
import ml_dtypes
import numpy as np
from jax import lax
from jax.experimental import pallas as pl
from jax.experimental.pallas import tpu as pltpu
from jax.sharding import PartitionSpec as P

SPAN = 64
CORNER = 8
LOW = 16
NY, NZ = 4, 12
N_DP = 96
N_OUTER = 8
VMEM = pl.BlockSpec(memory_space=pltpu.VMEM)
SMEM = pl.BlockSpec(memory_space=pltpu.SMEM)


def device_of(y, z, core):
    return ((y % NY) * NZ + z % NZ) * 2 + core


def shift(dz=0, dcore=0):
    return [
        (device_of(y, z, c), device_of(y, z + dz * (1 - 2 * c), c ^ dcore))
        for y in range(NY)
        for z in range(NZ)
        for c in range(2)
    ]


def far_groups():
    return [
        [device_of(y, 4 * q + s, c) for y in range(NY) for q in range(3)]
        for s in range(4)
        for c in range(2)
    ]


def halves(table):
    high = table.astype(ml_dtypes.bfloat16)
    low = (table - high.astype(np.float64)).astype(ml_dtypes.bfloat16)
    return high, low


def left_three(table):
    high, low = halves(table)
    return np.concatenate([high, low, high], axis=1)


def right_three(table):
    high, low = halves(table)
    return np.concatenate([high, low, high], axis=0)


def tables():
    k = np.arange(SPAN)[:, None]
    n = np.arange(SPAN)[None, :]
    scale = np.where(k == 0, math.sqrt(1.0 / SPAN), math.sqrt(2.0 / SPAN))
    low = (scale * np.cos(np.pi * (2 * n + 1) * k / (2.0 * SPAN)))[:LOW]
    left = np.zeros((2, 2, LOW, 2, 32))
    for h in range(2):
        for b in range(2):
            left[h, b, :, b, :] = low[:, h::2]
    left = left.reshape(64, 64)
    right = np.zeros((4, 128, 128))
    for g in range(4):
        right[g, :, 16 * g : 16 * g + 16] = np.concatenate([low.T, low.T], axis=0)
    right = right.reshape(512, 128)
    return left_three(left), right_three(right), left_three(left.T), right_three(right.T)


def chunk(y, q, kind, core):
    return pl.multiple_of(((y * NZ + 4 * q + kind) * 2 + core) * 64, 64)


def place():
    me = lax.axis_index("dp")
    core = lax.rem(me, 2)
    z = lax.rem(me // 2, NZ)
    return core, [lax.rem(z + d, 4) for d in (2, 1 + 2 * core, 3 - 2 * core, 0)]


def arrange_kernel(grads, send, square):
    core, kinds = place()

    def spread(i, carry):
        rows = pl.multiple_of(i * 16, 16)
        for first in range(0, 32, 8):
            wide = grads[0, 0, pl.ds(rows, 16), first * 128 : (first + 8) * 128]
            wide = wide.astype(jnp.float32)
            for side in (0, 8):
                turned = wide[side : side + 8].reshape(8, 8, 128)
                for r in range(8):
                    start = pl.multiple_of((rows + side + r) * 32 + first, 8)
                    square[pl.ds(start, 8), :] = turned[r]
        return carry

    lax.fori_loop(0, 12, spread, 0)

    def deal(i, carry):
        y, q = i // 3, lax.rem(i, 3)
        for slot, kind in enumerate((kinds[0], kinds[2], kinds[1], kinds[3])):
            send[slot, i] = square[pl.ds(chunk(y, q, kind, 1 - core), 64), :]
        return carry

    lax.fori_loop(0, 12, deal, 0)


def arrange(grads):
    shapes = [(4, 12, 64, 128), (6144, 128)]
    return pl.pallas_call(
        arrange_kernel,
        out_shape=tuple(jax.ShapeDtypeStruct(s, jnp.float32) for s in shapes),
        in_specs=[VMEM],
        out_specs=(VMEM, VMEM),
        compiler_params=pltpu.CompilerParams(vmem_limit_bytes=24 << 20),
    )(grads)


def chip_kernel(square, other, far, first, second, here):
    core, kinds = place()

    def add(i, carry):
        y, q = i // 3, lax.rem(i, 3)
        for slot, ref in enumerate((far, first, second, here)):
            mine = square[pl.ds(chunk(y, q, kinds[slot], core), 64), :]
            ref[i] = mine + other[slot, i]
        return carry

    lax.fori_loop(0, 12, add, 0)


def dot(a, b):
    return jnp.dot(a, b, preferred_element_type=jnp.float32)


def split(value):
    high = value.astype(jnp.bfloat16)
    low = (value - high.astype(jnp.float32)).astype(jnp.bfloat16)
    return high, low


def dot_left(table, value):
    high, low = split(value)
    return dot(table, jnp.concatenate([high, high, low], axis=0))


def dot_right(value, table):
    high, low = split(value)
    return dot(jnp.concatenate([high, high, low], axis=1), table)


def kept_kernel(parts, momentum, corner, left, right, moment, kept, copies, square):
    for t in range(32):
        square[pl.ds(t, 2, stride=32), :] = momentum[0, :, t * 128 : (t + 1) * 128]
    total = parts[0]
    for k in range(1, 12):
        total = total + parts[k]
    value = 0.9 * square[...] + total / N_DP
    moment[...] = value
    mixed = dot_left(left[...], value)
    lane = lax.broadcasted_iota(jnp.int32, (32, 128), 1)
    half = jnp.where(lane < SPAN, mixed[:32], mixed[32:])
    wide = jnp.concatenate([half[8 * g : 8 * g + 8] for g in range(4)], axis=1)
    low = dot_right(wide, right[...])
    row = lax.broadcasted_iota(jnp.int32, (8, 128), 0)
    lane = lax.broadcasted_iota(jnp.int32, (8, 128), 1)
    first = lane < 2 * LOW
    above = row + 8 * ((lane // LOW) % 2) - jnp.where(first, corner[0, 0], corner[1, 0])
    beside = lane % LOW - jnp.where(first, corner[0, 1], corner[1, 1])
    inside = (above >= 0) & (above < CORNER) & (beside >= 0) & (beside < CORNER)
    pack = jnp.where(inside & (lane < 4 * LOW), low, 0.0)
    kept[...] = pack
    for p in range(N_OUTER):
        copies[p] = pack


def last_kernel(moment, kept, packed, left_t, right_t, out, update, square, other):
    shared = packed[0]
    for p in range(1, N_OUTER):
        shared = shared + packed[p]
    both = jnp.concatenate([kept[...], shared / N_OUTER], axis=0)
    wide = dot_right(both, right_t[...])
    row = lax.broadcasted_iota(jnp.int32, (64, 128), 0)
    lane = lax.broadcasted_iota(jnp.int32, (64, 128), 1)
    same = (row < 32) == (lane < SPAN)
    sides = []
    for first in (0, 8):
        tall = [wide[first : first + 8, 128 * g : 128 * g + 128] for g in range(4)]
        sides.append(jnp.where(same, jnp.concatenate(tall + tall, axis=0), 0.0))
    back = dot_left(left_t[...], jnp.concatenate(sides, axis=1))
    square[...] = moment[...] - back[:, :128]
    other[...] = back[:, 128:]
    for t in range(32):
        out[0, :, t * 128 : (t + 1) * 128] = square[pl.ds(t, 2, stride=32), :]
        update[:, t * 128 : (t + 1) * 128] = other[pl.ds(t, 2, stride=32), :]


def call(kernel, out_shapes, args, scratch=(), smem=()):
    return pl.pallas_call(
        kernel,
        out_shape=tuple(jax.ShapeDtypeStruct(s, jnp.float32) for s in out_shapes),
        in_specs=[SMEM if i in smem else VMEM for i in range(len(args))],
        out_specs=tuple(VMEM for _ in out_shapes),
        scratch_shapes=[pltpu.VMEM(s, jnp.float32) for s in scratch],
        compiler_params=pltpu.CompilerParams(vmem_limit_bytes=24 << 20),
    )(*args)


def exchange(value, axis, groups=None):
    return lax.all_to_all(value, axis, 0, 0, axis_index_groups=groups, tiled=True)


def on_device(grads, momentum, corner):
    left, right, left_t, right_t = (jnp.asarray(v) for v in tables())
    tile = (64, 128)
    send, square = arrange(grads)
    other = lax.ppermute(send, "dp", shift(dcore=1))
    far, first, second, here = call(chip_kernel, [(12, 64, 128)] * 4, (square, other))
    zero = lax.ppermute(far, "dp", shift(dz=2))
    one = lax.ppermute(first, "dp", shift(dz=1))
    two = lax.ppermute(second, "dp", shift(dz=-1))
    parts = exchange(here + one + two + zero, "dp", far_groups())
    moment, kept, copies = call(
        kept_kernel,
        [tile, (8, 128), (N_OUTER, 8, 128)],
        (parts, momentum, corner, left, right),
        [tile],
        smem=(2,),
    )
    packed = exchange(copies, "outer")
    return call(
        last_kernel,
        [(1, 2, 4096), (2, 4096)],
        (moment, kept, packed, left_t, right_t),
        [tile, tile],
    )


def solution(mesh):
    in_specs = (P("outer", "dp", None, None), P("outer", "dp", None), P("dp", None))
    out_specs = (P("outer", "dp", None), P("dp", None))
    return jax.shard_map(
        on_device, mesh=mesh, in_specs=in_specs, out_specs=out_specs, check_vma=False
    )
```

```python
import math

import jax
import jax.numpy as jnp
import ml_dtypes
import numpy as np
from jax import lax
from jax.experimental import pallas as pl
from jax.experimental.pallas import tpu as pltpu
from jax.sharding import PartitionSpec as P

SPAN = 64
CORNER = 8
LOW = 16
NY, NZ = 4, 12
N_DP = 96
N_OUTER = 8
VMEM = pl.BlockSpec(memory_space=pltpu.VMEM)
SMEM = pl.BlockSpec(memory_space=pltpu.SMEM)


def device_of(y, z, core):
    return ((y % NY) * NZ + z % NZ) * 2 + core


def shift(dz=0, dcore=0):
    return [
        (device_of(y, z, c), device_of(y, z + dz * (1 - 2 * c), c ^ dcore))
        for y in range(NY)
        for z in range(NZ)
        for c in range(2)
    ]


def far_groups():
    return [
        [device_of(y, 4 * q + s, c) for y in range(NY) for q in range(3)][:: 1 - 2 * c]
        for s in range(4)
        for c in range(2)
    ]


def halves(table):
    high = table.astype(ml_dtypes.bfloat16)
    low = (table - high.astype(np.float64)).astype(ml_dtypes.bfloat16)
    return high, low


def left_three(table):
    high, low = halves(table)
    return np.concatenate([high, low, high], axis=1)


def right_three(table):
    high, low = halves(table)
    return np.concatenate([high, low, high], axis=0)


def tables():
    k = np.arange(SPAN)[:, None]
    n = np.arange(SPAN)[None, :]
    scale = np.where(k == 0, math.sqrt(1.0 / SPAN), math.sqrt(2.0 / SPAN))
    low = (scale * np.cos(np.pi * (2 * n + 1) * k / (2.0 * SPAN)))[:LOW]
    left = np.zeros((2, 2, LOW, 2, 32))
    for h in range(2):
        for b in range(2):
            left[h, b, :, b, :] = low[:, h::2]
    left = left.reshape(64, 64)
    right = np.zeros((4, 128, 128))
    for g in range(4):
        right[g, :, 16 * g : 16 * g + 16] = np.concatenate([low.T, low.T], axis=0)
    right = right.reshape(512, 128)
    return left_three(left), right_three(right), left_three(left.T), right_three(right.T)


def chunk(y, q, kind, core):
    return pl.multiple_of(((y * NZ + 4 * q + kind) * 2 + core) * 64, 64)


def member(i, core):
    i = i + core * (11 - 2 * i)
    return i // 3, lax.rem(i, 3)


def place():
    me = lax.axis_index("dp")
    core = lax.rem(me, 2)
    z = lax.rem(me // 2, NZ)
    return core, [lax.rem(z + d, 4) for d in (2, 1 + 2 * core, 3 - 2 * core, 0)]


def arrange_kernel(grads, send, square):
    core, kinds = place()

    def spread(i, carry):
        rows = pl.multiple_of(i * 16, 16)
        for first in range(0, 32, 8):
            wide = grads[0, 0, pl.ds(rows, 16), first * 128 : (first + 8) * 128]
            wide = wide.astype(jnp.float32)
            for side in (0, 8):
                turned = wide[side : side + 8].reshape(8, 8, 128)
                for r in range(8):
                    start = pl.multiple_of((rows + side + r) * 32 + first, 8)
                    square[pl.ds(start, 8), :] = turned[r]
        return carry

    lax.fori_loop(0, 12, spread, 0)

    def deal(i, carry):
        y, q = member(i, 1 - core)
        for slot, kind in enumerate((kinds[0], kinds[2], kinds[1], kinds[3])):
            send[slot, i] = square[pl.ds(chunk(y, q, kind, 1 - core), 64), :]
        return carry

    lax.fori_loop(0, 12, deal, 0)


def arrange(grads):
    shapes = [(4, 12, 64, 128), (6144, 128)]
    return pl.pallas_call(
        arrange_kernel,
        out_shape=tuple(jax.ShapeDtypeStruct(s, jnp.float32) for s in shapes),
        in_specs=[VMEM],
        out_specs=(VMEM, VMEM),
        compiler_params=pltpu.CompilerParams(vmem_limit_bytes=24 << 20),
    )(grads)


def chip_kernel(square, other, far, first, second, here):
    core, kinds = place()

    def add(i, carry):
        y, q = member(i, core)
        for slot, ref in enumerate((far, first, second, here)):
            mine = square[pl.ds(chunk(y, q, kinds[slot], core), 64), :]
            ref[i] = mine + other[slot, i]
        return carry

    lax.fori_loop(0, 12, add, 0)


def dot(a, b):
    return jnp.dot(a, b, preferred_element_type=jnp.float32)


def split(value):
    high = value.astype(jnp.bfloat16)
    low = (value - high.astype(jnp.float32)).astype(jnp.bfloat16)
    return high, low


def dot_left(table, value):
    high, low = split(value)
    return dot(table, jnp.concatenate([high, high, low], axis=0))


def dot_right(value, table):
    high, low = split(value)
    return dot(jnp.concatenate([high, high, low], axis=1), table)


def kept_kernel(parts, momentum, corner, left, right, moment, kept, copies, square):
    for t in range(32):
        square[pl.ds(t, 2, stride=32), :] = momentum[0, :, t * 128 : (t + 1) * 128]
    total = parts[0]
    for k in range(1, 12):
        total = total + parts[k]
    value = 0.9 * square[...] + total / N_DP
    moment[...] = value
    mixed = dot_left(left[...], value)
    lane = lax.broadcasted_iota(jnp.int32, (32, 128), 1)
    half = jnp.where(lane < SPAN, mixed[:32], mixed[32:])
    wide = jnp.concatenate([half[8 * g : 8 * g + 8] for g in range(4)], axis=1)
    low = dot_right(wide, right[...])
    row = lax.broadcasted_iota(jnp.int32, (8, 128), 0)
    lane = lax.broadcasted_iota(jnp.int32, (8, 128), 1)
    first = lane < 2 * LOW
    above = row + 8 * ((lane // LOW) % 2) - jnp.where(first, corner[0, 0], corner[1, 0])
    beside = lane % LOW - jnp.where(first, corner[0, 1], corner[1, 1])
    inside = (above >= 0) & (above < CORNER) & (beside >= 0) & (beside < CORNER)
    pack = jnp.where(inside & (lane < 4 * LOW), low, 0.0)
    kept[...] = pack
    for p in range(N_OUTER):
        copies[p] = pack


def last_kernel(moment, kept, packed, left_t, right_t, out, update, square, other):
    shared = packed[0]
    for p in range(1, N_OUTER):
        shared = shared + packed[p]
    both = jnp.concatenate([kept[...], shared / N_OUTER], axis=0)
    wide = dot_right(both, right_t[...])
    row = lax.broadcasted_iota(jnp.int32, (64, 128), 0)
    lane = lax.broadcasted_iota(jnp.int32, (64, 128), 1)
    same = (row < 32) == (lane < SPAN)
    sides = []
    for first in (0, 8):
        tall = [wide[first : first + 8, 128 * g : 128 * g + 128] for g in range(4)]
        sides.append(jnp.where(same, jnp.concatenate(tall + tall, axis=0), 0.0))
    back = dot_left(left_t[...], jnp.concatenate(sides, axis=1))
    square[...] = moment[...] - back[:, :128]
    other[...] = back[:, 128:]
    for t in range(32):
        out[0, :, t * 128 : (t + 1) * 128] = square[pl.ds(t, 2, stride=32), :]
        update[:, t * 128 : (t + 1) * 128] = other[pl.ds(t, 2, stride=32), :]


def call(kernel, out_shapes, args, scratch=(), smem=()):
    return pl.pallas_call(
        kernel,
        out_shape=tuple(jax.ShapeDtypeStruct(s, jnp.float32) for s in out_shapes),
        in_specs=[SMEM if i in smem else VMEM for i in range(len(args))],
        out_specs=tuple(VMEM for _ in out_shapes),
        scratch_shapes=[pltpu.VMEM(s, jnp.float32) for s in scratch],
        compiler_params=pltpu.CompilerParams(vmem_limit_bytes=24 << 20),
    )(*args)


def exchange(value, axis, groups=None):
    return lax.all_to_all(value, axis, 0, 0, axis_index_groups=groups, tiled=True)


def on_device(grads, momentum, corner):
    left, right, left_t, right_t = (jnp.asarray(v) for v in tables())
    tile = (64, 128)
    send, square = arrange(grads)
    other = lax.ppermute(send, "dp", shift(dcore=1))
    far, first, second, here = call(chip_kernel, [(12, 64, 128)] * 4, (square, other))
    zero = lax.ppermute(far, "dp", shift(dz=2))
    one = lax.ppermute(first, "dp", shift(dz=1))
    two = lax.ppermute(second, "dp", shift(dz=-1))
    parts = exchange(here + one + two + zero, "dp", far_groups())
    moment, kept, copies = call(
        kept_kernel,
        [tile, (8, 128), (N_OUTER, 8, 128)],
        (parts, momentum, corner, left, right),
        [tile],
        smem=(2,),
    )
    packed = exchange(copies, "outer")
    return call(
        last_kernel,
        [(1, 2, 4096), (2, 4096)],
        (moment, kept, packed, left_t, right_t),
        [tile, tile],
    )


def solution(mesh):
    in_specs = (P("outer", "dp", None, None), P("outer", "dp", None), P("dp", None))
    out_specs = (P("outer", "dp", None), P("dp", None))
    return jax.shard_map(
        on_device, mesh=mesh, in_specs=in_specs, out_specs=out_specs, check_vma=False
    )
```

```python
import math

import jax
import jax.numpy as jnp
import ml_dtypes
import numpy as np
from jax import lax
from jax.experimental import pallas as pl
from jax.experimental.pallas import tpu as pltpu
from jax.sharding import PartitionSpec as P

SPAN = 64
CORNER = 8
LOW = 16
NY, NZ = 4, 12
N_DP = 96
N_OUTER = 8
VMEM = pl.BlockSpec(memory_space=pltpu.VMEM)
SMEM = pl.BlockSpec(memory_space=pltpu.SMEM)


def device_of(y, z, core):
    return ((y % NY) * NZ + z % NZ) * 2 + core


def shift(dz=0, dcore=0):
    return [
        (device_of(y, z, c), device_of(y, z + dz * (1 - 2 * c), c ^ dcore))
        for y in range(NY)
        for z in range(NZ)
        for c in range(2)
    ]


def far_order(core):
    by_z = [(y, q) for q in range(3) for y in range(NY)]
    return by_z[::-1] if core else by_z


def far_groups():
    return [
        [device_of(y, 4 * q + s, c) for y, q in far_order(c)]
        for s in range(4)
        for c in range(2)
    ]


def halves(table):
    high = table.astype(ml_dtypes.bfloat16)
    low = (table - high.astype(np.float64)).astype(ml_dtypes.bfloat16)
    return high, low


def left_three(table):
    high, low = halves(table)
    return np.concatenate([high, low, high], axis=1)


def right_three(table):
    high, low = halves(table)
    return np.concatenate([high, low, high], axis=0)


def tables():
    k = np.arange(SPAN)[:, None]
    n = np.arange(SPAN)[None, :]
    scale = np.where(k == 0, math.sqrt(1.0 / SPAN), math.sqrt(2.0 / SPAN))
    low = (scale * np.cos(np.pi * (2 * n + 1) * k / (2.0 * SPAN)))[:LOW]
    left = np.zeros((2, 2, LOW, 2, 32))
    for h in range(2):
        for b in range(2):
            left[h, b, :, b, :] = low[:, h::2]
    left = left.reshape(64, 64)
    right = np.zeros((4, 128, 128))
    for g in range(4):
        right[g, :, 16 * g : 16 * g + 16] = np.concatenate([low.T, low.T], axis=0)
    right = right.reshape(512, 128)
    return left_three(left), right_three(right), left_three(left.T), right_three(right.T)


def chunk(y, q, kind, core):
    return pl.multiple_of(((y * NZ + 4 * q + kind) * 2 + core) * 64, 64)


def member(i, core):
    i = i + core * (11 - 2 * i)
    return lax.rem(i, 4), i // 4


def place():
    me = lax.axis_index("dp")
    core = lax.rem(me, 2)
    z = lax.rem(me // 2, NZ)
    return core, [lax.rem(z + d, 4) for d in (2, 1 + 2 * core, 3 - 2 * core, 0)]


def arrange_kernel(grads, send, square):
    core, kinds = place()

    def spread(i, carry):
        rows = pl.multiple_of(i * 16, 16)
        for first in range(0, 32, 8):
            wide = grads[0, 0, pl.ds(rows, 16), first * 128 : (first + 8) * 128]
            wide = wide.astype(jnp.float32)
            for side in (0, 8):
                turned = wide[side : side + 8].reshape(8, 8, 128)
                for r in range(8):
                    start = pl.multiple_of((rows + side + r) * 32 + first, 8)
                    square[pl.ds(start, 8), :] = turned[r]
        return carry

    lax.fori_loop(0, 12, spread, 0)

    def deal(i, carry):
        y, q = member(i, 1 - core)
        for slot, kind in enumerate((kinds[0], kinds[2], kinds[1], kinds[3])):
            send[slot, i] = square[pl.ds(chunk(y, q, kind, 1 - core), 64), :]
        return carry

    lax.fori_loop(0, 12, deal, 0)


def arrange(grads):
    shapes = [(4, 12, 64, 128), (6144, 128)]
    return pl.pallas_call(
        arrange_kernel,
        out_shape=tuple(jax.ShapeDtypeStruct(s, jnp.float32) for s in shapes),
        in_specs=[VMEM],
        out_specs=(VMEM, VMEM),
        compiler_params=pltpu.CompilerParams(vmem_limit_bytes=24 << 20),
    )(grads)


def chip_kernel(square, other, far, first, second, here):
    core, kinds = place()

    def add(i, carry):
        y, q = member(i, core)
        for slot, ref in enumerate((far, first, second, here)):
            mine = square[pl.ds(chunk(y, q, kinds[slot], core), 64), :]
            ref[i] = mine + other[slot, i]
        return carry

    lax.fori_loop(0, 12, add, 0)


def dot(a, b):
    return jnp.dot(a, b, preferred_element_type=jnp.float32)


def split(value):
    high = value.astype(jnp.bfloat16)
    low = (value - high.astype(jnp.float32)).astype(jnp.bfloat16)
    return high, low


def dot_left(table, value):
    high, low = split(value)
    return dot(table, jnp.concatenate([high, high, low], axis=0))


def dot_right(value, table):
    high, low = split(value)
    return dot(jnp.concatenate([high, high, low], axis=1), table)


def kept_kernel(parts, momentum, corner, left, right, moment, kept, copies, square):
    for t in range(32):
        square[pl.ds(t, 2, stride=32), :] = momentum[0, :, t * 128 : (t + 1) * 128]
    total = parts[0]
    for k in range(1, 12):
        total = total + parts[k]
    value = 0.9 * square[...] + total / N_DP
    moment[...] = value
    mixed = dot_left(left[...], value)
    lane = lax.broadcasted_iota(jnp.int32, (32, 128), 1)
    half = jnp.where(lane < SPAN, mixed[:32], mixed[32:])
    wide = jnp.concatenate([half[8 * g : 8 * g + 8] for g in range(4)], axis=1)
    low = dot_right(wide, right[...])
    row = lax.broadcasted_iota(jnp.int32, (8, 128), 0)
    lane = lax.broadcasted_iota(jnp.int32, (8, 128), 1)
    first = lane < 2 * LOW
    above = row + 8 * ((lane // LOW) % 2) - jnp.where(first, corner[0, 0], corner[1, 0])
    beside = lane % LOW - jnp.where(first, corner[0, 1], corner[1, 1])
    inside = (above >= 0) & (above < CORNER) & (beside >= 0) & (beside < CORNER)
    pack = jnp.where(inside & (lane < 4 * LOW), low, 0.0)
    kept[...] = pack
    for p in range(N_OUTER):
        copies[p] = pack


def last_kernel(moment, kept, packed, left_t, right_t, out, update, square, other):
    shared = packed[0]
    for p in range(1, N_OUTER):
        shared = shared + packed[p]
    both = jnp.concatenate([kept[...], shared / N_OUTER], axis=0)
    wide = dot_right(both, right_t[...])
    row = lax.broadcasted_iota(jnp.int32, (64, 128), 0)
    lane = lax.broadcasted_iota(jnp.int32, (64, 128), 1)
    same = (row < 32) == (lane < SPAN)
    sides = []
    for first in (0, 8):
        tall = [wide[first : first + 8, 128 * g : 128 * g + 128] for g in range(4)]
        sides.append(jnp.where(same, jnp.concatenate(tall + tall, axis=0), 0.0))
    back = dot_left(left_t[...], jnp.concatenate(sides, axis=1))
    square[...] = moment[...] - back[:, :128]
    other[...] = back[:, 128:]
    for t in range(32):
        out[0, :, t * 128 : (t + 1) * 128] = square[pl.ds(t, 2, stride=32), :]
        update[:, t * 128 : (t + 1) * 128] = other[pl.ds(t, 2, stride=32), :]


def call(kernel, out_shapes, args, scratch=(), smem=()):
    return pl.pallas_call(
        kernel,
        out_shape=tuple(jax.ShapeDtypeStruct(s, jnp.float32) for s in out_shapes),
        in_specs=[SMEM if i in smem else VMEM for i in range(len(args))],
        out_specs=tuple(VMEM for _ in out_shapes),
        scratch_shapes=[pltpu.VMEM(s, jnp.float32) for s in scratch],
        compiler_params=pltpu.CompilerParams(vmem_limit_bytes=24 << 20),
    )(*args)


def exchange(value, axis, groups=None):
    return lax.all_to_all(value, axis, 0, 0, axis_index_groups=groups, tiled=True)


def on_device(grads, momentum, corner):
    left, right, left_t, right_t = (jnp.asarray(v) for v in tables())
    tile = (64, 128)
    send, square = arrange(grads)
    other = lax.ppermute(send, "dp", shift(dcore=1))
    far, first, second, here = call(chip_kernel, [(12, 64, 128)] * 4, (square, other))
    zero = lax.ppermute(far, "dp", shift(dz=2))
    one = lax.ppermute(first, "dp", shift(dz=1))
    two = lax.ppermute(second, "dp", shift(dz=-1))
    parts = exchange(here + one + two + zero, "dp", far_groups())
    moment, kept, copies = call(
        kept_kernel,
        [tile, (8, 128), (N_OUTER, 8, 128)],
        (parts, momentum, corner, left, right),
        [tile],
        smem=(2,),
    )
    packed = exchange(copies, "outer")
    return call(
        last_kernel,
        [(1, 2, 4096), (2, 4096)],
        (moment, kept, packed, left_t, right_t),
        [tile, tile],
    )


def solution(mesh):
    in_specs = (P("outer", "dp", None, None), P("outer", "dp", None), P("dp", None))
    out_specs = (P("outer", "dp", None), P("dp", None))
    return jax.shard_map(
        on_device, mesh=mesh, in_specs=in_specs, out_specs=out_specs, check_vma=False
    )
```
